32 devices in a mesh: groups: 2 (over y), owner: 8 (over z, x), tile: 2 (over core).
Axes of the slice: x: 2, y: 2, z: 4, core: 2. Of those that a mesh axis runs over, the one named last changes fastest.
Arguments:
- embeddings: bfloat16 [8192, 1024], P(('groups', 'owner', 'tile')), parts along dimension 0, may hold values from -6 to 6
- cluster_of: int32 [8192], P(('groups', 'owner', 'tile')), parts along dimension 0, may hold values from 0 to 15, as said below
- rank_of: int32 [8192], P(('groups', 'owner', 'tile')), parts along dimension 0, may hold values from 0 to 511, as said below
Outputs:
- max_similarity: float32 [8192], P(('groups', 'owner', 'tile')), parts along dimension 0
The draws below stay inside these ranges and needn't reach their ends.
There are 2 independent parts, one for each index of `groups`. The reference program is written for one: setup_inputs(seed, part) draws one part's arguments, and reference() takes and returns one part's arrays. A program takes and returns all parts, laid end to end along the dimension named above; each array names one. Nothing has to cross between parts.
Inputs may be any that keep to these rules, and one draw needn't show every extreme that they name: `cluster_of`: in each aligned block of 256 rows (the rows of one device) no cluster is named more than 32 times; one cluster is named exactly 32 times in every block, so that it holds 512 rows. `rank_of`: within each cluster the ranks of its rows are 0 to its size minus 1, each once; cluster ids, ranks and sizes as given by cluster_of.
All inputs are finite; a program needn't handle non-finite values.
Results may differ from the reference program's by a relative error of at most 0.0013.
Values may be sent and summed in bfloat16 or wider, within the bound.
A program may use at most 64 MiB of HBM per device.

```python
import jax
import jax.numpy as jnp
from jax import lax

D = 1024
ROW_DEV = 256
CLUSTERS = 16
CAP = 32
MAXC = 512
ROWS = 4096


def shared_clusters(key):
    device_count = ROWS // ROW_DEV
    slot_count = CLUSTERS * CAP
    subkeys = jax.random.split(key, 5)
    cluster_weight = jax.random.randint(subkeys[0], (CLUSTERS,), 1, 5)
    giant_cluster = jax.random.randint(subkeys[1], (), 0, CLUSTERS)
    slot_cluster = jnp.arange(slot_count, dtype=jnp.int32) // CAP
    raw_score = jax.random.randint(subkeys[2], (device_count, slot_count), 0, 8192) * cluster_weight[slot_cluster]
    raw_score = raw_score + jnp.where(slot_cluster == giant_cluster, 32768, 0)[None, :]
    slot_score = raw_score * slot_count + jnp.arange(slot_count, dtype=jnp.int32)[None, :]
    unused, chosen = lax.top_k(slot_score, ROW_DEV)
    shuffle_key = jax.random.randint(subkeys[3], (device_count, ROW_DEV), 0, 4096) * ROW_DEV + jnp.arange(ROW_DEV, dtype=jnp.int32)[None, :]
    row_order = jnp.argsort(shuffle_key, axis=1)
    chosen = jnp.take_along_axis(chosen, row_order, axis=1)
    cluster_ids = (chosen // CAP).reshape(ROWS).astype(jnp.int32)
    priority = jax.random.permutation(subkeys[4], ROWS).astype(jnp.int32)
    combined = cluster_ids * ROWS + priority
    sorted_rows = jnp.argsort(combined)
    position = jnp.zeros((ROWS,), jnp.int32).at[sorted_rows].set(jnp.arange(ROWS, dtype=jnp.int32))
    counts = jnp.zeros((CLUSTERS,), jnp.int32).at[cluster_ids].add(1)
    first_rank = jnp.cumsum(counts) - counts
    rank_ids = position - first_rank[cluster_ids]
    return (cluster_ids, rank_ids.astype(jnp.int32))


def draw_cluster_of(key, part):
    cluster_ids, rank_ids = shared_clusters(key)
    return cluster_ids


def draw_rank_of(key, part):
    cluster_ids, rank_ids = shared_clusters(key)
    return rank_ids


def steps_of(key, dims, cuts, least, top_value):
    loudness = 1.0
    for dim, parts in cuts:
        heights = jax.random.uniform(jax.random.fold_in(jax.random.fold_in(key, 6), dim), (parts,), jnp.float32, least / len(cuts), top_value / len(cuts))
        loudness = loudness * jnp.repeat(jnp.exp(heights), dims[dim] // parts).reshape((-1,) + (1,) * (len(dims) - 1 - dim))
    return loudness


def normal_values(stream_key, extent, spread, reach, shards=(), kind=jnp.bfloat16):
    array = spread * jax.random.normal(stream_key, extent, jnp.float32)
    if shards:
        array = array * steps_of(stream_key, extent, shards, -0.22, 0.18)
    return jnp.clip(array, -reach, reach).astype(kind)


def setup_inputs(seed: int = 0, part: int = 0) -> dict:
    keys = jax.random.split(jax.random.key(seed), 4)
    part_splits = jax.random.split(jax.random.fold_in(keys[3], part), 4)
    return {
        "embeddings": normal_values(part_splits[0], (ROWS, D), 1.0, 6.0, ((0, 16),)),
        "cluster_of": draw_cluster_of(jax.random.fold_in(jax.random.fold_in(keys[3], part), 71), part),
        "rank_of": draw_rank_of(jax.random.fold_in(jax.random.fold_in(keys[3], part), 71), part),
    }


EPSILON = 1e-06

def normalize_rows(embeddings):
    as_float = embeddings.astype(jnp.float32)
    total = lax.optimization_barrier(jnp.sum(as_float * as_float, axis=1, keepdims=True))
    return (as_float * lax.rsqrt(total + EPSILON)).astype(jnp.bfloat16)

def reference(embeddings, cluster_of, rank_of):
    normed = normalize_rows(embeddings)
    row_ids = jnp.arange(ROWS, dtype=jnp.int32)
    lookup_table = jnp.full((CLUSTERS, MAXC), ROWS, dtype=jnp.int32).at[cluster_of, rank_of].set(row_ids)
    padded = jnp.concatenate([normed, jnp.zeros((1, D), normed.dtype)], axis=0)
    positions = jnp.arange(MAXC, dtype=jnp.int32)
    earlier_mask = positions[None, :] < positions[:, None]

    def per_cluster(indices):
        members = padded[indices]
        scores = jnp.dot(members, members.T, preferred_element_type=jnp.float32)
        return lax.optimization_barrier(jnp.max(jnp.where(earlier_mask, scores, -1.0), axis=1))
    maxima = lax.map(per_cluster, lookup_table)
    return maxima[cluster_of, rank_of]
```

```python
import functools

import jax
import jax.numpy as jnp
from jax import lax
from jax.experimental import pallas as pl
from jax.experimental.pallas import tpu as pltpu
from jax.sharding import PartitionSpec as P

MESH = pl.DeviceIdType.MESH
EPSILON = 1e-06
LANES = 128


def flip(value, mask):
    bit = 1
    while bit <= mask:
        if mask & bit:
            value = value + bit * (1 - 2 * ((value // bit) % 2))
        bit *= 2
    return value


def cluster_kernel(
    count,
    capacity,
    emb_ref,
    cluster_ref,
    rank_ref,
    out_ref,
    send_rows,
    rows,
    send_ranks,
    ranks,
    send_best,
    best,
    row_send_sem,
    row_recv_sem,
    rank_send_sem,
    rank_recv_sem,
    best_send_sem,
    best_recv_sem,
):
    row_count, width = emb_ref.shape
    slots = count * capacity
    per = LANES // capacity
    owner = lax.axis_index("owner")
    core = lax.axis_index("tile")
    me = owner * 2 + core

    def peer(k):
        return {"owner": flip(owner, k // 2), "tile": flip(core, k % 2)}

    barrier = pltpu.get_barrier_semaphore()
    for k in range(1, count):
        pl.semaphore_signal(barrier, inc=1, device_id=peer(k), device_id_type=MESH)

    cluster = cluster_ref[...].reshape(1, row_count)
    rank = rank_ref[...].reshape(1, row_count)
    distance = cluster ^ me
    member = distance == lax.broadcasted_iota(jnp.int32, (count, row_count), 0)
    member_f = member.astype(jnp.float32)
    member_b = member_f.astype(jnp.bfloat16)
    before = (
        lax.broadcasted_iota(jnp.int32, (row_count, row_count), 0)
        < lax.broadcasted_iota(jnp.int32, (row_count, row_count), 1)
    ).astype(jnp.float32).astype(jnp.bfloat16)
    seen = jnp.dot(member_b, before, preferred_element_type=jnp.float32)
    occurrence = jnp.sum(seen * member_f, axis=0, keepdims=True).astype(jnp.int32)
    slot = distance * capacity + occurrence

    lane_of = (slot % LANES) == lax.broadcasted_iota(jnp.int32, (LANES, row_count), 0)
    lane_b = lane_of.astype(jnp.float32).astype(jnp.bfloat16)
    high = (rank // 16 - slots // 16).astype(jnp.float32)
    low = (rank % 16).astype(jnp.float32)
    nt = (((1,), (1,)), ((), ()))
    rank_high = lax.dot_general(
        (member_f * high).astype(jnp.bfloat16), lane_b, nt, preferred_element_type=jnp.float32
    )
    rank_low = lax.dot_general(
        (member_f * low).astype(jnp.bfloat16), lane_b, nt, preferred_element_type=jnp.float32
    )
    rank_rows = 16.0 * rank_high + rank_low
    for k in range(count):
        send_ranks[k] = rank_rows[k : k + 1, :]
    ranks[0] = rank_rows[0:1, :]

    values = emb_ref[...].astype(jnp.float32)
    total = jnp.sum(values * values, axis=1, keepdims=True)
    normed = (values * lax.rsqrt(total + EPSILON)).astype(jnp.bfloat16)

    def place(first, size):
        chosen = slot == first + lax.broadcasted_iota(jnp.int32, (size, row_count), 0)
        chosen = chosen.astype(jnp.float32).astype(jnp.bfloat16)
        return jnp.dot(chosen, normed, preferred_element_type=jnp.float32).astype(jnp.bfloat16)

    def row_copy(k):
        here = pl.ds(k * capacity, capacity)
        return pltpu.make_async_remote_copy(
            src_ref=send_rows.at[here],
            dst_ref=rows.at[here],
            send_sem=row_send_sem.at[k],
            recv_sem=row_recv_sem.at[k],
            device_id=peer(k),
            device_id_type=MESH,
        )

    def rank_copy(k):
        return pltpu.make_async_remote_copy(
            src_ref=send_ranks.at[k],
            dst_ref=ranks.at[k],
            send_sem=rank_send_sem.at[k],
            recv_sem=rank_recv_sem.at[k],
            device_id=peer(k),
            device_id_type=MESH,
        )

    def best_copy(k):
        return pltpu.make_async_remote_copy(
            src_ref=send_best.at[k // per],
            dst_ref=best.at[k],
            send_sem=best_send_sem.at[k],
            recv_sem=best_recv_sem.at[k],
            device_id=peer(k),
            device_id_type=MESH,
        )

    half = slots // 2
    send_rows[half:] = place(half, half)
    pl.semaphore_wait(barrier, count - 1)
    for k in range(count - 1, count // 2 - 1, -1):
        row_copy(k).start()
    for k in range(1, count):
        rank_copy(k).start()
    near = place(0, half)
    send_rows[:half] = near
    for k in range(count // 2 - 1, 0, -1):
        row_copy(k).start()
    rows[:capacity] = near[:capacity]

    for k in range(1, count):
        rank_copy(k).wait_recv()
    blocks = slots // LANES
    rank_lanes = jnp.concatenate(
        [
            sum(ranks[b * per + j] for j in range(per)) + float(slots)
            for b in range(blocks)
        ],
        axis=0,
    )
    padded = jnp.concatenate([rank_lanes, jnp.zeros((LANES - blocks, LANES), jnp.float32)], axis=0)
    turned = jnp.transpose(padded)

    for k in range(1, count):
        row_copy(k).wait_recv()
    for q in range(blocks):
        queries = rows[pl.ds(q * LANES, LANES)]
        query_rank = rank_lanes[q : q + 1, :]
        top = jnp.full((1, LANES), -1.0, jnp.float32)
        scores = lax.dot_general(rows[...], queries, nt, preferred_element_type=jnp.float32)
        for b in range(blocks):
            part = scores[b * LANES : (b + 1) * LANES]
            earlier = turned[:, b : b + 1] < query_rank
            top = jnp.maximum(
                top, jnp.max(jnp.where(earlier, part, -1.0), axis=0, keepdims=True)
            )
        send_best[q] = top
        for k in range(q * per, (q + 1) * per):
            if k:
                best_copy(k).start()
            else:
                best[0] = top

    for k in range(1, count):
        best_copy(k).wait_recv()
    answers = jnp.concatenate([best[k] for k in range(count)], axis=0)
    spread = lax.dot_general(
        jnp.transpose(answers),
        member_f,
        (((1,), (0,)), ((), ())),
        precision=lax.Precision.HIGHEST,
        preferred_element_type=jnp.float32,
    )
    picked = jnp.sum(jnp.where(lane_of, spread, 0.0), axis=0, keepdims=True)
    out_ref[...] = picked.reshape(row_count)

    for k in range(1, count):
        row_copy(k).wait_send()
        rank_copy(k).wait_send()
        best_copy(k).wait_send()


def fused(embeddings, cluster_of, rank_of, count):
    row_count, width = embeddings.shape
    capacity = 2 * row_count // count
    slots = count * capacity
    vmem = pl.BlockSpec(memory_space=pltpu.VMEM)
    return pl.pallas_call(
        functools.partial(cluster_kernel, count, capacity),
        out_shape=jax.ShapeDtypeStruct((row_count,), jnp.float32),
        in_specs=[vmem] * 3,
        out_specs=vmem,
        scratch_shapes=[
            pltpu.VMEM((slots, width), jnp.bfloat16),
            pltpu.VMEM((slots, width), jnp.bfloat16),
            pltpu.VMEM((count, 1, LANES), jnp.float32),
            pltpu.VMEM((count, 1, LANES), jnp.float32),
            pltpu.VMEM((slots // LANES, 1, LANES), jnp.float32),
            pltpu.VMEM((count, 1, LANES), jnp.float32),
        ]
        + [pltpu.SemaphoreType.DMA((count,))] * 6,
        compiler_params=pltpu.CompilerParams(
            collective_id=0, has_side_effects=True, vmem_limit_bytes=32 * 1024 * 1024
        ),
    )(embeddings, cluster_of, rank_of)


CL_OWN = 2


def normalize_rows(embeddings):
    as_float = embeddings.astype(jnp.float32)
    total = jnp.sum(as_float * as_float, axis=1, keepdims=True)
    return (as_float * lax.rsqrt(total + EPSILON)).astype(jnp.bfloat16)


def place_rows(arrived_rows, arrived_ranks, longest):
    local_count = arrived_rows.shape[1]
    feature_width = arrived_rows.shape[3]
    cluster_index = jnp.broadcast_to(
        jnp.arange(local_count, dtype=jnp.int32)[None, :, None], arrived_ranks.shape
    )
    ordered = jnp.zeros((local_count, longest, feature_width), jnp.bfloat16)
    ordered = ordered.at[cluster_index, arrived_ranks].set(arrived_rows, mode="drop")
    live_rows = jnp.sum((arrived_ranks < longest).astype(jnp.int32), axis=(0, 2))
    return (ordered, live_rows)


def lookup_maxima(maxima, ranks, longest):
    cluster_index = jnp.broadcast_to(
        jnp.arange(maxima.shape[0], dtype=jnp.int32)[None, :, None], ranks.shape
    )
    return maxima[cluster_index, jnp.minimum(ranks, longest - 1)]


def block_maxima(ordered_rows, first, count, block_rows):
    query_rows = lax.dynamic_slice_in_dim(ordered_rows, 0 + first, count, 0)
    scores = jnp.einsum("qd,kd->qk", query_rows, ordered_rows, preferred_element_type=jnp.float32)
    query_pos = 0 + first + jnp.arange(count, dtype=jnp.int32)
    key_pos = jnp.arange(block_rows, dtype=jnp.int32)
    masked = jnp.where(key_pos[None, :] < query_pos[:, None], scores, -1.0)
    row_best = jnp.max(masked, axis=1)
    results = [row_best]
    return jnp.stack(results)


def exchanged(embeddings, cluster_of, rank_of):
    row_count, feature_width = embeddings.shape
    owner_count = lax.axis_size("owner")
    core_count = lax.axis_size("tile")
    cluster_count = CL_OWN * owner_count
    capacity = 2 * row_count // cluster_count
    longest = owner_count * core_count * capacity
    block_rows = 512
    normed = normalize_rows(embeddings)
    member = (cluster_of[:, None] == jnp.arange(cluster_count, dtype=jnp.int32)[None, :]).astype(
        jnp.bfloat16
    )
    row_ids = jnp.arange(row_count, dtype=jnp.int32)
    earlier = (row_ids[:, None] > row_ids[None, :]).astype(jnp.bfloat16)
    seen = jnp.dot(earlier, member, preferred_element_type=jnp.float32)
    occurrence = jnp.sum(seen * member.astype(jnp.float32), axis=1).astype(jnp.int32)
    slot_index = cluster_of * capacity + occurrence
    outgoing = (
        jnp.zeros((cluster_count * capacity, feature_width), jnp.bfloat16)
        .at[slot_index]
        .set(normed)
    )
    outgoing_ranks = (
        jnp.full((cluster_count * capacity,), longest, jnp.int32).at[slot_index].set(rank_of)
    )
    outgoing = outgoing.reshape(owner_count, CL_OWN, capacity, feature_width)
    outgoing_ranks = outgoing_ranks.reshape(owner_count, CL_OWN, capacity)
    arrived, arrived_ranks = (
        lax.all_to_all(outgoing, "owner", split_axis=0, concat_axis=0, tiled=True),
        lax.all_to_all(outgoing_ranks, "owner", split_axis=0, concat_axis=0, tiled=True),
    )
    everything, every_rank = (
        lax.all_gather(arrived, "tile", axis=0, tiled=True),
        lax.all_gather(arrived_ranks, "tile", axis=0, tiled=True),
    )
    ordered, live_rows = place_rows(everything, every_rank, longest)
    share = block_rows // core_count
    first = lax.axis_index("tile") * share
    halves = jnp.stack(
        [
            block_maxima(ordered[local_index], first, share, block_rows)
            for local_index in range(CL_OWN)
        ]
    )
    whole = lax.all_gather(halves[:, :, None, :], "tile", axis=2, tiled=True)
    maxima = whole.reshape(CL_OWN, longest)
    answers = lookup_maxima(maxima, arrived_ranks, longest)
    returned = lax.all_to_all(answers, "owner", split_axis=0, concat_axis=0, tiled=True)
    return returned.reshape(cluster_count * capacity)[slot_index]


def local(embeddings, cluster_of, rank_of):
    count = lax.axis_size("owner") * lax.axis_size("tile")
    if (2 * embeddings.shape[0] // count) % 16 == 0:
        return fused(embeddings, cluster_of, rank_of, count)
    return exchanged(embeddings, cluster_of, rank_of)


def solution(mesh):
    in_specs = (
        P(("groups", "owner", "tile"), None),
        P(("groups", "owner", "tile")),
        P(("groups", "owner", "tile")),
    )
    out_specs = P(("groups", "owner", "tile"))
    return jax.shard_map(local, mesh=mesh, in_specs=in_specs, out_specs=out_specs, check_vma=False)
```

```python
import functools

import jax
import jax.numpy as jnp
from jax import lax
from jax.experimental import pallas as pl
from jax.experimental.pallas import tpu as pltpu
from jax.sharding import PartitionSpec as P

MESH = pl.DeviceIdType.MESH
EPSILON = 1e-06
LANES = 128


def flip(value, mask):
    bit = 1
    while bit <= mask:
        if mask & bit:
            value = value + bit * (1 - 2 * ((value // bit) % 2))
        bit *= 2
    return value


def cluster_kernel(
    count,
    capacity,
    emb_hbm,
    cluster_hbm,
    rank_hbm,
    out_ref,
    emb_ref,
    cluster_ref,
    rank_ref,
    send_rows,
    rows,
    normed,
    send_ranks,
    ranks,
    send_best,
    best,
    load_sem,
    row_send_sem,
    row_recv_sem,
    rank_send_sem,
    rank_recv_sem,
    best_send_sem,
    best_recv_sem,
):
    row_count, width = emb_ref.shape
    slots = count * capacity
    per = LANES // capacity
    blocks = slots // LANES
    owner = lax.axis_index("owner")
    core = lax.axis_index("tile")
    me = owner * 2 + core

    def peer(k):
        return {"owner": flip(owner, k // 2), "tile": flip(core, k % 2)}

    loads = [
        pltpu.make_async_copy(source, target, load_sem.at[i])
        for i, (source, target) in enumerate(
            [(cluster_hbm, cluster_ref), (rank_hbm, rank_ref), (emb_hbm, emb_ref)]
        )
    ]
    for load in loads:
        load.start()
    barrier = pltpu.get_barrier_semaphore()
    for k in range(count - 1, 0, -1):
        pl.semaphore_signal(barrier, inc=1, device_id=peer(k), device_id_type=MESH)

    loads[0].wait()
    cluster = cluster_ref[...].reshape(1, row_count)
    distance = cluster ^ me
    member = distance == lax.broadcasted_iota(jnp.int32, (count, row_count), 0)
    member_f = member.astype(jnp.float32)
    member_b = member_f.astype(jnp.bfloat16)
    before = (
        (
            lax.broadcasted_iota(jnp.int32, (row_count, row_count), 0)
            < lax.broadcasted_iota(jnp.int32, (row_count, row_count), 1)
        )
        .astype(jnp.float32)
        .astype(jnp.bfloat16)
    )
    seen = jnp.dot(member_b, before, preferred_element_type=jnp.float32)
    occurrence = jnp.sum(seen * member_f, axis=0, keepdims=True).astype(jnp.int32)
    slot = distance * capacity + occurrence
    nt = (((1,), (1,)), ((), ()))

    def block_rows(b, n=1):
        return pl.ds(b * LANES, n * LANES)

    def place(b, n=1):
        size = n * LANES
        chosen = slot == b * LANES + lax.broadcasted_iota(jnp.int32, (size, row_count), 0)
        chosen = chosen.astype(jnp.float32).astype(jnp.bfloat16)
        placed = jnp.dot(chosen, emb_ref[...], preferred_element_type=jnp.float32)
        send_rows[block_rows(b, n)] = placed.astype(jnp.bfloat16)

    def row_copy(k):
        here = pl.ds(k * capacity, capacity)
        return pltpu.make_async_remote_copy(
            src_ref=send_rows.at[here],
            dst_ref=rows.at[here],
            send_sem=row_send_sem.at[k],
            recv_sem=row_recv_sem.at[k],
            device_id=peer(k),
            device_id_type=MESH,
        )

    def rank_copy(k):
        return pltpu.make_async_remote_copy(
            src_ref=send_ranks.at[k],
            dst_ref=ranks.at[k],
            send_sem=rank_send_sem.at[k],
            recv_sem=rank_recv_sem.at[k],
            device_id=peer(k),
            device_id_type=MESH,
        )

    def best_copy(k):
        return pltpu.make_async_remote_copy(
            src_ref=send_best.at[k // per],
            dst_ref=best.at[k],
            send_sem=best_send_sem.at[k],
            recv_sem=best_recv_sem.at[k],
            device_id=peer(k),
            device_id_type=MESH,
        )

    def start_rows(b):
        for k in range((b + 1) * per - 1, b * per - 1, -1):
            if k:
                row_copy(k).start()

    loads[2].wait()
    place(blocks - 1)
    pl.semaphore_wait(barrier, count - 1)
    start_rows(blocks - 1)
    place(blocks - 2)
    start_rows(blocks - 2)

    loads[1].wait()
    rank = rank_ref[...].reshape(1, row_count)
    lane_of = (slot % LANES) == lax.broadcasted_iota(jnp.int32, (LANES, row_count), 0)
    lane_b = lane_of.astype(jnp.float32).astype(jnp.bfloat16)
    high = (rank // 16 - slots // 16).astype(jnp.float32)
    low = (rank % 16).astype(jnp.float32)
    rank_high = lax.dot_general(
        (member_f * high).astype(jnp.bfloat16), lane_b, nt, preferred_element_type=jnp.float32
    )
    rank_low = lax.dot_general(
        (member_f * low).astype(jnp.bfloat16), lane_b, nt, preferred_element_type=jnp.float32
    )
    rank_rows = 16.0 * rank_high + rank_low
    for k in range(count):
        send_ranks[k] = rank_rows[k : k + 1, :]
    for k in range(count - 1, 0, -1):
        rank_copy(k).start()
    ranks[0] = rank_rows[0:1, :]

    place(0, blocks - 2)
    for b in range(blocks - 3, -1, -1):
        start_rows(b)
    rows[:capacity] = send_rows[:capacity]

    def arrive(b, n=1):
        for k in range((b + n) * per - 1, b * per - 1, -1):
            if k:
                row_copy(k).wait_recv()
        values = rows[block_rows(b, n)].astype(jnp.float32)
        total = jnp.sum(values * values, axis=1, keepdims=True)
        normed[block_rows(b, n)] = (values * lax.rsqrt(total + EPSILON)).astype(jnp.bfloat16)

    for k in range(1, count):
        rank_copy(k).wait_recv()
    rank_lanes = [
        sum(ranks[b * per + j] for j in range(per)) + float(slots) for b in range(blocks)
    ]
    turned = jnp.transpose(
        jnp.concatenate(rank_lanes + [jnp.zeros((LANES - blocks, LANES), jnp.float32)], axis=0)
    )
    tops = [jnp.full((1, LANES), -1.0, jnp.float32) for _ in range(blocks)]

    def score(first_key, keys, first_query, queries):
        scores = lax.dot_general(
            normed[block_rows(first_key, keys)],
            normed[block_rows(first_query, queries)],
            nt,
            preferred_element_type=jnp.float32,
        )
        for q in range(queries):
            for b in range(keys):
                part = scores[b * LANES : (b + 1) * LANES, q * LANES : (q + 1) * LANES]
                key = first_key + b
                query = first_query + q
                earlier = turned[:, key : key + 1] < rank_lanes[query]
                found = jnp.max(jnp.where(earlier, part, -1.0), axis=0, keepdims=True)
                tops[query] = jnp.maximum(tops[query], found)

    def answer(b):
        send_best[b] = tops[b]
        for k in range((b + 1) * per - 1, b * per - 1, -1):
            if k:
                best_copy(k).start()
            else:
                best[0] = tops[b]

    near = blocks - 2
    arrive(0, near)
    score(0, near, 0, near)
    arrive(near + 1)
    score(0, near, near + 1, 1)
    score(near + 1, 1, near + 1, 1)
    score(near + 1, 1, 0, near)
    arrive(near)
    score(near, 1, near + 1, 1)
    answer(near + 1)
    score(0, blocks, near, 1)
    answer(near)
    score(near, 1, 0, near)
    for b in range(near - 1, -1, -1):
        answer(b)

    for k in range(1, count):
        row_copy(k).wait_send()
        rank_copy(k).wait_send()
    for k in range(1, count):
        best_copy(k).wait_recv()
    answers = jnp.concatenate([best[k] for k in range(count)], axis=0)
    spread = lax.dot_general(
        jnp.transpose(answers),
        member_f,
        (((1,), (0,)), ((), ())),
        precision=lax.Precision.HIGHEST,
        preferred_element_type=jnp.float32,
    )
    picked = jnp.sum(jnp.where(lane_of, spread, 0.0), axis=0, keepdims=True)
    out_ref[...] = picked.reshape(row_count)
    for k in range(1, count):
        best_copy(k).wait_send()


def fused(embeddings, cluster_of, rank_of, count):
    row_count, width = embeddings.shape
    capacity = 2 * row_count // count
    slots = count * capacity
    return pl.pallas_call(
        functools.partial(cluster_kernel, count, capacity),
        out_shape=jax.ShapeDtypeStruct((row_count,), jnp.float32),
        in_specs=[pl.BlockSpec(memory_space=pl.ANY)] * 3,
        out_specs=pl.BlockSpec(memory_space=pltpu.VMEM),
        scratch_shapes=[
            pltpu.VMEM((row_count, width), jnp.bfloat16),
            pltpu.VMEM((row_count,), jnp.int32),
            pltpu.VMEM((row_count,), jnp.int32),
            pltpu.VMEM((slots, width), jnp.bfloat16),
            pltpu.VMEM((slots, width), jnp.bfloat16),
            pltpu.VMEM((slots, width), jnp.bfloat16),
            pltpu.VMEM((count, 1, LANES), jnp.float32),
            pltpu.VMEM((count, 1, LANES), jnp.float32),
            pltpu.VMEM((slots // LANES, 1, LANES), jnp.float32),
            pltpu.VMEM((count, 1, LANES), jnp.float32),
            pltpu.SemaphoreType.DMA((3,)),
        ]
        + [pltpu.SemaphoreType.DMA((count,))] * 6,
        compiler_params=pltpu.CompilerParams(
            collective_id=0, has_side_effects=True, vmem_limit_bytes=48 * 1024 * 1024
        ),
    )(embeddings, cluster_of, rank_of)


CL_OWN = 2


def normalize_rows(embeddings):
    as_float = embeddings.astype(jnp.float32)
    total = jnp.sum(as_float * as_float, axis=1, keepdims=True)
    return (as_float * lax.rsqrt(total + EPSILON)).astype(jnp.bfloat16)


def place_rows(arrived_rows, arrived_ranks, longest):
    local_count = arrived_rows.shape[1]
    feature_width = arrived_rows.shape[3]
    cluster_index = jnp.broadcast_to(
        jnp.arange(local_count, dtype=jnp.int32)[None, :, None], arrived_ranks.shape
    )
    ordered = jnp.zeros((local_count, longest, feature_width), jnp.bfloat16)
    ordered = ordered.at[cluster_index, arrived_ranks].set(arrived_rows, mode="drop")
    live_rows = jnp.sum((arrived_ranks < longest).astype(jnp.int32), axis=(0, 2))
    return (ordered, live_rows)


def lookup_maxima(maxima, ranks, longest):
    cluster_index = jnp.broadcast_to(
        jnp.arange(maxima.shape[0], dtype=jnp.int32)[None, :, None], ranks.shape
    )
    return maxima[cluster_index, jnp.minimum(ranks, longest - 1)]


def block_maxima(ordered_rows, first, count, block_rows):
    query_rows = lax.dynamic_slice_in_dim(ordered_rows, 0 + first, count, 0)
    scores = jnp.einsum("qd,kd->qk", query_rows, ordered_rows, preferred_element_type=jnp.float32)
    query_pos = 0 + first + jnp.arange(count, dtype=jnp.int32)
    key_pos = jnp.arange(block_rows, dtype=jnp.int32)
    masked = jnp.where(key_pos[None, :] < query_pos[:, None], scores, -1.0)
    row_best = jnp.max(masked, axis=1)
    results = [row_best]
    return jnp.stack(results)


def exchanged(embeddings, cluster_of, rank_of):
    row_count, feature_width = embeddings.shape
    owner_count = lax.axis_size("owner")
    core_count = lax.axis_size("tile")
    cluster_count = CL_OWN * owner_count
    capacity = 2 * row_count // cluster_count
    longest = owner_count * core_count * capacity
    block_rows = 512
    normed = normalize_rows(embeddings)
    member = (cluster_of[:, None] == jnp.arange(cluster_count, dtype=jnp.int32)[None, :]).astype(
        jnp.bfloat16
    )
    row_ids = jnp.arange(row_count, dtype=jnp.int32)
    earlier = (row_ids[:, None] > row_ids[None, :]).astype(jnp.bfloat16)
    seen = jnp.dot(earlier, member, preferred_element_type=jnp.float32)
    occurrence = jnp.sum(seen * member.astype(jnp.float32), axis=1).astype(jnp.int32)
    slot_index = cluster_of * capacity + occurrence
    outgoing = (
        jnp.zeros((cluster_count * capacity, feature_width), jnp.bfloat16)
        .at[slot_index]
        .set(normed)
    )
    outgoing_ranks = (
        jnp.full((cluster_count * capacity,), longest, jnp.int32).at[slot_index].set(rank_of)
    )
    outgoing = outgoing.reshape(owner_count, CL_OWN, capacity, feature_width)
    outgoing_ranks = outgoing_ranks.reshape(owner_count, CL_OWN, capacity)
    arrived, arrived_ranks = (
        lax.all_to_all(outgoing, "owner", split_axis=0, concat_axis=0, tiled=True),
        lax.all_to_all(outgoing_ranks, "owner", split_axis=0, concat_axis=0, tiled=True),
    )
    everything, every_rank = (
        lax.all_gather(arrived, "tile", axis=0, tiled=True),
        lax.all_gather(arrived_ranks, "tile", axis=0, tiled=True),
    )
    ordered, live_rows = place_rows(everything, every_rank, longest)
    share = block_rows // core_count
    first = lax.axis_index("tile") * share
    halves = jnp.stack(
        [
            block_maxima(ordered[local_index], first, share, block_rows)
            for local_index in range(CL_OWN)
        ]
    )
    whole = lax.all_gather(halves[:, :, None, :], "tile", axis=2, tiled=True)
    maxima = whole.reshape(CL_OWN, longest)
    answers = lookup_maxima(maxima, arrived_ranks, longest)
    returned = lax.all_to_all(answers, "owner", split_axis=0, concat_axis=0, tiled=True)
    return returned.reshape(cluster_count * capacity)[slot_index]


def local(embeddings, cluster_of, rank_of):
    count = lax.axis_size("owner") * lax.axis_size("tile")
    if (2 * embeddings.shape[0] // count) % 16 == 0:
        return fused(embeddings, cluster_of, rank_of, count)
    return exchanged(embeddings, cluster_of, rank_of)


def solution(mesh):
    in_specs = (
        P(("groups", "owner", "tile"), None),
        P(("groups", "owner", "tile")),
        P(("groups", "owner", "tile")),
    )
    out_specs = P(("groups", "owner", "tile"))
    return jax.shard_map(local, mesh=mesh, in_specs=in_specs, out_specs=out_specs, check_vma=False)
```

```python
import functools

import jax
import jax.numpy as jnp
from jax import lax
from jax.experimental import pallas as pl
from jax.experimental.pallas import tpu as pltpu
from jax.sharding import PartitionSpec as P

MESH = pl.DeviceIdType.MESH
EPSILON = 1e-06
LANES = 128


def flip(value, mask):
    bit = 1
    while bit <= mask:
        if mask & bit:
            value = value + bit * (1 - 2 * ((value // bit) % 2))
        bit *= 2
    return value


def cluster_kernel(
    count,
    capacity,
    emb_hbm,
    cluster_hbm,
    rank_hbm,
    out_ref,
    emb_ref,
    cluster_ref,
    rank_ref,
    send_rows,
    rows,
    normed,
    send_ranks,
    ranks,
    send_best,
    best,
    load_sem,
    row_send_sem,
    row_recv_sem,
    rank_send_sem,
    rank_recv_sem,
    best_send_sem,
    best_recv_sem,
):
    row_count, width = emb_ref.shape
    slots = count * capacity
    per = LANES // capacity
    blocks = slots // LANES
    owner = lax.axis_index("owner")
    core = lax.axis_index("tile")
    me = owner * 2 + core

    def peer(k):
        return {"owner": flip(owner, k // 2), "tile": flip(core, k % 2)}

    loads = [
        pltpu.make_async_copy(source, target, load_sem.at[i])
        for i, (source, target) in enumerate(
            [(cluster_hbm, cluster_ref), (rank_hbm, rank_ref), (emb_hbm, emb_ref)]
        )
    ]
    for load in loads:
        load.start()
    barrier = pltpu.get_barrier_semaphore()
    for k in range(count - 1, 0, -1):
        pl.semaphore_signal(barrier, inc=1, device_id=peer(k), device_id_type=MESH)

    loads[0].wait()
    cluster = cluster_ref[...].reshape(1, row_count)
    distance = cluster ^ me
    member = distance == lax.broadcasted_iota(jnp.int32, (count, row_count), 0)
    member_f = member.astype(jnp.float32)
    member_b = member_f.astype(jnp.bfloat16)
    before = (
        (
            lax.broadcasted_iota(jnp.int32, (row_count, row_count), 0)
            < lax.broadcasted_iota(jnp.int32, (row_count, row_count), 1)
        )
        .astype(jnp.float32)
        .astype(jnp.bfloat16)
    )
    seen = jnp.dot(member_b, before, preferred_element_type=jnp.float32)
    occurrence = jnp.sum(seen * member_f, axis=0, keepdims=True).astype(jnp.int32)
    slot = distance * capacity + occurrence
    nt = (((1,), (1,)), ((), ()))

    def block_rows(b, n=1):
        return pl.ds(b * LANES, n * LANES)

    def place(b, n=1):
        size = n * LANES
        chosen = slot == b * LANES + lax.broadcasted_iota(jnp.int32, (size, row_count), 0)
        chosen = chosen.astype(jnp.float32).astype(jnp.bfloat16)
        placed = jnp.dot(chosen, emb_ref[...], preferred_element_type=jnp.float32)
        send_rows[block_rows(b, n)] = placed.astype(jnp.bfloat16)

    def row_copy(k):
        here = pl.ds(k * capacity, capacity)
        return pltpu.make_async_remote_copy(
            src_ref=send_rows.at[here],
            dst_ref=rows.at[here],
            send_sem=row_send_sem.at[k],
            recv_sem=row_recv_sem.at[k],
            device_id=peer(k),
            device_id_type=MESH,
        )

    def rank_copy(k):
        return pltpu.make_async_remote_copy(
            src_ref=send_ranks.at[k],
            dst_ref=ranks.at[k],
            send_sem=rank_send_sem.at[k],
            recv_sem=rank_recv_sem.at[k],
            device_id=peer(k),
            device_id_type=MESH,
        )

    def best_copy(k):
        return pltpu.make_async_remote_copy(
            src_ref=send_best.at[k // per],
            dst_ref=best.at[k],
            send_sem=best_send_sem.at[k],
            recv_sem=best_recv_sem.at[k],
            device_id=peer(k),
            device_id_type=MESH,
        )

    def start_rows(b):
        for k in range((b + 1) * per - 1, b * per - 1, -1):
            if k:
                row_copy(k).start()

    loads[1].wait()
    rank = rank_ref[...].reshape(1, row_count)
    lane_of = (slot % LANES) == lax.broadcasted_iota(jnp.int32, (LANES, row_count), 0)
    lane_b = lane_of.astype(jnp.float32).astype(jnp.bfloat16)
    high = (rank // 16 - slots // 16).astype(jnp.float32)
    low = (rank % 16).astype(jnp.float32)
    rank_high = lax.dot_general(
        (member_f * high).astype(jnp.bfloat16), lane_b, nt, preferred_element_type=jnp.float32
    )
    rank_low = lax.dot_general(
        (member_f * low).astype(jnp.bfloat16), lane_b, nt, preferred_element_type=jnp.float32
    )
    rank_rows = 16.0 * rank_high + rank_low
    for k in range(count):
        send_ranks[k] = rank_rows[k : k + 1, :]
    ranks[0] = rank_rows[0:1, :]

    loads[2].wait()
    place(blocks - 1)
    pl.semaphore_wait(barrier, count - 1)
    for k in range(count - 1, 0, -1):
        rank_copy(k).start()
    start_rows(blocks - 1)
    place(blocks - 2)
    start_rows(blocks - 2)

    place(0, blocks - 2)
    for b in range(blocks - 3, -1, -1):
        start_rows(b)
    rows[:capacity] = send_rows[:capacity]

    def arrive(b, n=1):
        for k in range((b + n) * per - 1, b * per - 1, -1):
            if k:
                row_copy(k).wait_recv()
        values = rows[block_rows(b, n)].astype(jnp.float32)
        total = jnp.sum(values * values, axis=1, keepdims=True)
        normed[block_rows(b, n)] = (values * lax.rsqrt(total + EPSILON)).astype(jnp.bfloat16)

    for k in range(1, count):
        rank_copy(k).wait_recv()
    rank_lanes = [
        sum(ranks[b * per + j] for j in range(per)) + float(slots) for b in range(blocks)
    ]
    turned = jnp.transpose(
        jnp.concatenate(rank_lanes + [jnp.zeros((LANES - blocks, LANES), jnp.float32)], axis=0)
    )
    tops = [jnp.full((1, LANES), -1.0, jnp.float32) for _ in range(blocks)]

    def score(first_key, keys, first_query, queries):
        scores = lax.dot_general(
            normed[block_rows(first_key, keys)],
            normed[block_rows(first_query, queries)],
            nt,
            preferred_element_type=jnp.float32,
        )
        for q in range(queries):
            for b in range(keys):
                part = scores[b * LANES : (b + 1) * LANES, q * LANES : (q + 1) * LANES]
                key = first_key + b
                query = first_query + q
                earlier = turned[:, key : key + 1] < rank_lanes[query]
                found = jnp.max(jnp.where(earlier, part, -1.0), axis=0, keepdims=True)
                tops[query] = jnp.maximum(tops[query], found)

    def answer(b):
        send_best[b] = tops[b]
        for k in range((b + 1) * per - 1, b * per - 1, -1):
            if k:
                best_copy(k).start()
            else:
                best[0] = tops[b]

    near = blocks - 2
    arrive(0, near)
    score(0, near, 0, near)
    arrive(near + 1)
    score(0, near, near + 1, 1)
    score(near + 1, 1, near + 1, 1)
    score(near + 1, 1, 0, near)
    arrive(near)
    score(near, 1, near + 1, 1)
    answer(near + 1)
    score(0, blocks, near, 1)
    answer(near)
    score(near, 1, 0, near)
    for b in range(near - 1, -1, -1):
        answer(b)

    for k in range(1, count):
        row_copy(k).wait_send()
        rank_copy(k).wait_send()
    for k in range(1, count):
        best_copy(k).wait_recv()
    answers = jnp.concatenate([best[k] for k in range(count)], axis=0)
    spread = lax.dot_general(
        jnp.transpose(answers),
        member_f,
        (((1,), (0,)), ((), ())),
        precision=lax.Precision.HIGHEST,
        preferred_element_type=jnp.float32,
    )
    picked = jnp.sum(jnp.where(lane_of, spread, 0.0), axis=0, keepdims=True)
    out_ref[...] = picked.reshape(row_count)
    for k in range(1, count):
        best_copy(k).wait_send()


def fused(embeddings, cluster_of, rank_of, count):
    row_count, width = embeddings.shape
    capacity = 2 * row_count // count
    slots = count * capacity
    return pl.pallas_call(
        functools.partial(cluster_kernel, count, capacity),
        out_shape=jax.ShapeDtypeStruct((row_count,), jnp.float32),
        in_specs=[pl.BlockSpec(memory_space=pl.ANY)] * 3,
        out_specs=pl.BlockSpec(memory_space=pltpu.VMEM),
        scratch_shapes=[
            pltpu.VMEM((row_count, width), jnp.bfloat16),
            pltpu.VMEM((row_count,), jnp.int32),
            pltpu.VMEM((row_count,), jnp.int32),
            pltpu.VMEM((slots, width), jnp.bfloat16),
            pltpu.VMEM((slots, width), jnp.bfloat16),
            pltpu.VMEM((slots, width), jnp.bfloat16),
            pltpu.VMEM((count, 1, LANES), jnp.float32),
            pltpu.VMEM((count, 1, LANES), jnp.float32),
            pltpu.VMEM((slots // LANES, 1, LANES), jnp.float32),
            pltpu.VMEM((count, 1, LANES), jnp.float32),
            pltpu.SemaphoreType.DMA((3,)),
        ]
        + [pltpu.SemaphoreType.DMA((count,))] * 6,
        compiler_params=pltpu.CompilerParams(collective_id=0, has_side_effects=True),
    )(embeddings, cluster_of, rank_of)


CL_OWN = 2


def normalize_rows(embeddings):
    as_float = embeddings.astype(jnp.float32)
    total = jnp.sum(as_float * as_float, axis=1, keepdims=True)
    return (as_float * lax.rsqrt(total + EPSILON)).astype(jnp.bfloat16)


def place_rows(arrived_rows, arrived_ranks, longest):
    local_count = arrived_rows.shape[1]
    feature_width = arrived_rows.shape[3]
    cluster_index = jnp.broadcast_to(
        jnp.arange(local_count, dtype=jnp.int32)[None, :, None], arrived_ranks.shape
    )
    ordered = jnp.zeros((local_count, longest, feature_width), jnp.bfloat16)
    ordered = ordered.at[cluster_index, arrived_ranks].set(arrived_rows, mode="drop")
    live_rows = jnp.sum((arrived_ranks < longest).astype(jnp.int32), axis=(0, 2))
    return (ordered, live_rows)


def lookup_maxima(maxima, ranks, longest):
    cluster_index = jnp.broadcast_to(
        jnp.arange(maxima.shape[0], dtype=jnp.int32)[None, :, None], ranks.shape
    )
    return maxima[cluster_index, jnp.minimum(ranks, longest - 1)]


def block_maxima(ordered_rows, first, count, block_rows):
    query_rows = lax.dynamic_slice_in_dim(ordered_rows, 0 + first, count, 0)
    scores = jnp.einsum("qd,kd->qk", query_rows, ordered_rows, preferred_element_type=jnp.float32)
    query_pos = 0 + first + jnp.arange(count, dtype=jnp.int32)
    key_pos = jnp.arange(block_rows, dtype=jnp.int32)
    masked = jnp.where(key_pos[None, :] < query_pos[:, None], scores, -1.0)
    row_best = jnp.max(masked, axis=1)
    results = [row_best]
    return jnp.stack(results)


def exchanged(embeddings, cluster_of, rank_of):
    row_count, feature_width = embeddings.shape
    owner_count = lax.axis_size("owner")
    core_count = lax.axis_size("tile")
    cluster_count = CL_OWN * owner_count
    capacity = 2 * row_count // cluster_count
    longest = owner_count * core_count * capacity
    block_rows = 512
    normed = normalize_rows(embeddings)
    member = (cluster_of[:, None] == jnp.arange(cluster_count, dtype=jnp.int32)[None, :]).astype(
        jnp.bfloat16
    )
    row_ids = jnp.arange(row_count, dtype=jnp.int32)
    earlier = (row_ids[:, None] > row_ids[None, :]).astype(jnp.bfloat16)
    seen = jnp.dot(earlier, member, preferred_element_type=jnp.float32)
    occurrence = jnp.sum(seen * member.astype(jnp.float32), axis=1).astype(jnp.int32)
    slot_index = cluster_of * capacity + occurrence
    outgoing = (
        jnp.zeros((cluster_count * capacity, feature_width), jnp.bfloat16)
        .at[slot_index]
        .set(normed)
    )
    outgoing_ranks = (
        jnp.full((cluster_count * capacity,), longest, jnp.int32).at[slot_index].set(rank_of)
    )
    outgoing = outgoing.reshape(owner_count, CL_OWN, capacity, feature_width)
    outgoing_ranks = outgoing_ranks.reshape(owner_count, CL_OWN, capacity)
    arrived, arrived_ranks = (
        lax.all_to_all(outgoing, "owner", split_axis=0, concat_axis=0, tiled=True),
        lax.all_to_all(outgoing_ranks, "owner", split_axis=0, concat_axis=0, tiled=True),
    )
    everything, every_rank = (
        lax.all_gather(arrived, "tile", axis=0, tiled=True),
        lax.all_gather(arrived_ranks, "tile", axis=0, tiled=True),
    )
    ordered, live_rows = place_rows(everything, every_rank, longest)
    share = block_rows // core_count
    first = lax.axis_index("tile") * share
    halves = jnp.stack(
        [
            block_maxima(ordered[local_index], first, share, block_rows)
            for local_index in range(CL_OWN)
        ]
    )
    whole = lax.all_gather(halves[:, :, None, :], "tile", axis=2, tiled=True)
    maxima = whole.reshape(CL_OWN, longest)
    answers = lookup_maxima(maxima, arrived_ranks, longest)
    returned = lax.all_to_all(answers, "owner", split_axis=0, concat_axis=0, tiled=True)
    return returned.reshape(cluster_count * capacity)[slot_index]


def local(embeddings, cluster_of, rank_of):
    count = lax.axis_size("owner") * lax.axis_size("tile")
    if (2 * embeddings.shape[0] // count) % 16 == 0:
        return fused(embeddings, cluster_of, rank_of, count)
    return exchanged(embeddings, cluster_of, rank_of)


def solution(mesh):
    in_specs = (
        P(("groups", "owner", "tile"), None),
        P(("groups", "owner", "tile")),
        P(("groups", "owner", "tile")),
    )
    out_specs = P(("groups", "owner", "tile"))
    return jax.shard_map(local, mesh=mesh, in_specs=in_specs, out_specs=out_specs, check_vma=False)
```

```python
import functools

import jax
import jax.numpy as jnp
from jax import lax
from jax.experimental import pallas as pl
from jax.experimental.pallas import tpu as pltpu
from jax.sharding import PartitionSpec as P

MESH = pl.DeviceIdType.MESH
EPSILON = 1e-06
LANES = 128


def flip(value, mask):
    bit = 1
    while bit <= mask:
        if mask & bit:
            value = value + bit * (1 - 2 * ((value // bit) % 2))
        bit *= 2
    return value


def cluster_kernel(
    count,
    capacity,
    emb_hbm,
    cluster_hbm,
    rank_hbm,
    out_ref,
    emb_ref,
    cluster_ref,
    rank_ref,
    send_rows,
    rows,
    normed,
    send_ranks,
    ranks,
    send_best,
    best,
    load_sem,
    row_send_sem,
    row_recv_sem,
    rank_send_sem,
    rank_recv_sem,
    best_send_sem,
    best_recv_sem,
):
    row_count, width = emb_ref.shape
    slots = count * capacity
    per = LANES // capacity
    blocks = slots // LANES
    owner = lax.axis_index("owner")
    core = lax.axis_index("tile")
    me = owner * 2 + core

    def peer(k):
        return {"owner": flip(owner, k // 2), "tile": flip(core, k % 2)}

    loads = [
        pltpu.make_async_copy(source, target, load_sem.at[i])
        for i, (source, target) in enumerate(
            [(cluster_hbm, cluster_ref), (rank_hbm, rank_ref), (emb_hbm, emb_ref)]
        )
    ]
    for load in loads:
        load.start()
    barrier = pltpu.get_barrier_semaphore()
    for k in range(count - 1, 0, -1):
        pl.semaphore_signal(barrier, inc=1, device_id=peer(k), device_id_type=MESH)

    loads[0].wait()
    cluster = cluster_ref[...].reshape(1, row_count)
    distance = cluster ^ me
    member = distance == lax.broadcasted_iota(jnp.int32, (count, row_count), 0)
    member_f = member.astype(jnp.float32)
    member_b = member_f.astype(jnp.bfloat16)
    before = (
        (
            lax.broadcasted_iota(jnp.int32, (row_count, row_count), 0)
            < lax.broadcasted_iota(jnp.int32, (row_count, row_count), 1)
        )
        .astype(jnp.float32)
        .astype(jnp.bfloat16)
    )
    seen = jnp.dot(member_b, before, preferred_element_type=jnp.float32)
    occurrence = jnp.sum(seen * member_f, axis=0, keepdims=True).astype(jnp.int32)
    slot = distance * capacity + occurrence
    nt = (((1,), (1,)), ((), ()))

    def block_rows(b, n=1):
        return pl.ds(b * LANES, n * LANES)

    def place(b, n=1):
        size = n * LANES
        chosen = slot == b * LANES + lax.broadcasted_iota(jnp.int32, (size, row_count), 0)
        chosen = chosen.astype(jnp.float32).astype(jnp.bfloat16)
        placed = jnp.dot(chosen, normed[...], preferred_element_type=jnp.float32)
        send_rows[block_rows(b, n)] = placed.astype(jnp.bfloat16)

    def row_copy(k):
        here = pl.ds(k * capacity, capacity)
        return pltpu.make_async_remote_copy(
            src_ref=send_rows.at[here],
            dst_ref=rows.at[here],
            send_sem=row_send_sem.at[k],
            recv_sem=row_recv_sem.at[k],
            device_id=peer(k),
            device_id_type=MESH,
        )

    def rank_copy(k):
        return pltpu.make_async_remote_copy(
            src_ref=send_ranks.at[k],
            dst_ref=ranks.at[k],
            send_sem=rank_send_sem.at[k],
            recv_sem=rank_recv_sem.at[k],
            device_id=peer(k),
            device_id_type=MESH,
        )

    def best_copy(k):
        return pltpu.make_async_remote_copy(
            src_ref=send_best.at[k // per],
            dst_ref=best.at[k],
            send_sem=best_send_sem.at[k],
            recv_sem=best_recv_sem.at[k],
            device_id=peer(k),
            device_id_type=MESH,
        )

    def start_rows(b):
        for k in range((b + 1) * per - 1, b * per - 1, -1):
            if k:
                row_copy(k).start()

    loads[1].wait()
    rank = rank_ref[...].reshape(1, row_count)
    lane_of = (slot % LANES) == lax.broadcasted_iota(jnp.int32, (LANES, row_count), 0)
    lane_b = lane_of.astype(jnp.float32).astype(jnp.bfloat16)
    high = (rank // 16 - slots // 16).astype(jnp.float32)
    low = (rank % 16).astype(jnp.float32)
    rank_high = lax.dot_general(
        (member_f * high).astype(jnp.bfloat16), lane_b, nt, preferred_element_type=jnp.float32
    )
    rank_low = lax.dot_general(
        (member_f * low).astype(jnp.bfloat16), lane_b, nt, preferred_element_type=jnp.float32
    )
    rank_rows = 16.0 * rank_high + rank_low
    for k in range(count):
        send_ranks[k] = rank_rows[k : k + 1, :]
    ranks[0] = rank_rows[0:1, :]

    loads[2].wait()
    values = emb_ref[...].astype(jnp.float32)
    total = jnp.sum(values * values, axis=1, keepdims=True)
    normed[...] = (values * lax.rsqrt(total + EPSILON)).astype(jnp.bfloat16)
    place(blocks - 1)
    pl.semaphore_wait(barrier, count - 1)
    for k in range(count - 1, 0, -1):
        rank_copy(k).start()
    place(blocks - 2)
    for j in range(per - 1, -1, -1):
        row_copy((blocks - 1) * per + j).start()
        row_copy((blocks - 2) * per + j).start()

    place(0, blocks - 2)
    for b in range(blocks - 3, -1, -1):
        start_rows(b)
    rows[:capacity] = send_rows[:capacity]

    def arrive(b, n=1):
        for k in range((b + n) * per - 1, b * per - 1, -1):
            if k:
                row_copy(k).wait_recv()

    for k in range(1, count):
        rank_copy(k).wait_recv()
    rank_lanes = [
        sum(ranks[b * per + j] for j in range(per)) + float(slots) for b in range(blocks)
    ]
    turned = jnp.transpose(
        jnp.concatenate(rank_lanes + [jnp.zeros((LANES - blocks, LANES), jnp.float32)], axis=0)
    )
    tops = [jnp.full((1, LANES), -1.0, jnp.float32) for _ in range(blocks)]

    def score(first_key, keys, first_query, queries):
        scores = lax.dot_general(
            rows[block_rows(first_key, keys)],
            rows[block_rows(first_query, queries)],
            nt,
            preferred_element_type=jnp.float32,
        )
        for q in range(queries):
            for b in range(keys):
                part = scores[b * LANES : (b + 1) * LANES, q * LANES : (q + 1) * LANES]
                key = first_key + b
                query = first_query + q
                earlier = turned[:, key : key + 1] < rank_lanes[query]
                found = jnp.max(jnp.where(earlier, part, -1.0), axis=0, keepdims=True)
                tops[query] = jnp.maximum(tops[query], found)

    def answer(b):
        send_best[b] = tops[b]
        for k in range((b + 1) * per - 1, b * per - 1, -1):
            if k:
                best_copy(k).start()
            else:
                best[0] = tops[b]

    near = blocks - 2
    arrive(0, near)
    score(0, near, 0, near)
    arrive(near + 1)
    score(0, near, near + 1, 1)
    score(near + 1, 1, near + 1, 1)
    score(near + 1, 1, 0, near)
    arrive(near)
    score(near, 1, near + 1, 1)
    answer(near + 1)
    score(0, blocks, near, 1)
    answer(near)
    score(near, 1, 0, near)
    for b in range(near - 1, -1, -1):
        answer(b)

    for k in range(1, count):
        row_copy(k).wait_send()
        rank_copy(k).wait_send()
    for k in range(1, count):
        best_copy(k).wait_recv()
    answers = jnp.concatenate([best[k] for k in range(count)], axis=0)
    spread = lax.dot_general(
        jnp.transpose(answers),
        member_f,
        (((1,), (0,)), ((), ())),
        precision=lax.Precision.HIGHEST,
        preferred_element_type=jnp.float32,
    )
    picked = jnp.sum(jnp.where(lane_of, spread, 0.0), axis=0, keepdims=True)
    out_ref[...] = picked.reshape(row_count)
    for k in range(1, count):
        best_copy(k).wait_send()


def fused(embeddings, cluster_of, rank_of, count):
    row_count, width = embeddings.shape
    capacity = 2 * row_count // count
    slots = count * capacity
    return pl.pallas_call(
        functools.partial(cluster_kernel, count, capacity),
        out_shape=jax.ShapeDtypeStruct((row_count,), jnp.float32),
        in_specs=[pl.BlockSpec(memory_space=pl.ANY)] * 3,
        out_specs=pl.BlockSpec(memory_space=pltpu.VMEM),
        scratch_shapes=[
            pltpu.VMEM((row_count, width), jnp.bfloat16),
            pltpu.VMEM((row_count,), jnp.int32),
            pltpu.VMEM((row_count,), jnp.int32),
            pltpu.VMEM((slots, width), jnp.bfloat16),
            pltpu.VMEM((slots, width), jnp.bfloat16),
            pltpu.VMEM((row_count, width), jnp.bfloat16),
            pltpu.VMEM((count, 1, LANES), jnp.float32),
            pltpu.VMEM((count, 1, LANES), jnp.float32),
            pltpu.VMEM((slots // LANES, 1, LANES), jnp.float32),
            pltpu.VMEM((count, 1, LANES), jnp.float32),
            pltpu.SemaphoreType.DMA((3,)),
        ]
        + [pltpu.SemaphoreType.DMA((count,))] * 6,
        compiler_params=pltpu.CompilerParams(collective_id=0, has_side_effects=True),
    )(embeddings, cluster_of, rank_of)


CL_OWN = 2


def normalize_rows(embeddings):
    as_float = embeddings.astype(jnp.float32)
    total = jnp.sum(as_float * as_float, axis=1, keepdims=True)
    return (as_float * lax.rsqrt(total + EPSILON)).astype(jnp.bfloat16)


def place_rows(arrived_rows, arrived_ranks, longest):
    local_count = arrived_rows.shape[1]
    feature_width = arrived_rows.shape[3]
    cluster_index = jnp.broadcast_to(
        jnp.arange(local_count, dtype=jnp.int32)[None, :, None], arrived_ranks.shape
    )
    ordered = jnp.zeros((local_count, longest, feature_width), jnp.bfloat16)
    ordered = ordered.at[cluster_index, arrived_ranks].set(arrived_rows, mode="drop")
    live_rows = jnp.sum((arrived_ranks < longest).astype(jnp.int32), axis=(0, 2))
    return (ordered, live_rows)


def lookup_maxima(maxima, ranks, longest):
    cluster_index = jnp.broadcast_to(
        jnp.arange(maxima.shape[0], dtype=jnp.int32)[None, :, None], ranks.shape
    )
    return maxima[cluster_index, jnp.minimum(ranks, longest - 1)]


def block_maxima(ordered_rows, first, count, block_rows):
    query_rows = lax.dynamic_slice_in_dim(ordered_rows, 0 + first, count, 0)
    scores = jnp.einsum("qd,kd->qk", query_rows, ordered_rows, preferred_element_type=jnp.float32)
    query_pos = 0 + first + jnp.arange(count, dtype=jnp.int32)
    key_pos = jnp.arange(block_rows, dtype=jnp.int32)
    masked = jnp.where(key_pos[None, :] < query_pos[:, None], scores, -1.0)
    row_best = jnp.max(masked, axis=1)
    results = [row_best]
    return jnp.stack(results)


def exchanged(embeddings, cluster_of, rank_of):
    row_count, feature_width = embeddings.shape
    owner_count = lax.axis_size("owner")
    core_count = lax.axis_size("tile")
    cluster_count = CL_OWN * owner_count
    capacity = 2 * row_count // cluster_count
    longest = owner_count * core_count * capacity
    block_rows = 512
    normed = normalize_rows(embeddings)
    member = (cluster_of[:, None] == jnp.arange(cluster_count, dtype=jnp.int32)[None, :]).astype(
        jnp.bfloat16
    )
    row_ids = jnp.arange(row_count, dtype=jnp.int32)
    earlier = (row_ids[:, None] > row_ids[None, :]).astype(jnp.bfloat16)
    seen = jnp.dot(earlier, member, preferred_element_type=jnp.float32)
    occurrence = jnp.sum(seen * member.astype(jnp.float32), axis=1).astype(jnp.int32)
    slot_index = cluster_of * capacity + occurrence
    outgoing = (
        jnp.zeros((cluster_count * capacity, feature_width), jnp.bfloat16)
        .at[slot_index]
        .set(normed)
    )
    outgoing_ranks = (
        jnp.full((cluster_count * capacity,), longest, jnp.int32).at[slot_index].set(rank_of)
    )
    outgoing = outgoing.reshape(owner_count, CL_OWN, capacity, feature_width)
    outgoing_ranks = outgoing_ranks.reshape(owner_count, CL_OWN, capacity)
    arrived, arrived_ranks = (
        lax.all_to_all(outgoing, "owner", split_axis=0, concat_axis=0, tiled=True),
        lax.all_to_all(outgoing_ranks, "owner", split_axis=0, concat_axis=0, tiled=True),
    )
    everything, every_rank = (
        lax.all_gather(arrived, "tile", axis=0, tiled=True),
        lax.all_gather(arrived_ranks, "tile", axis=0, tiled=True),
    )
    ordered, live_rows = place_rows(everything, every_rank, longest)
    share = block_rows // core_count
    first = lax.axis_index("tile") * share
    halves = jnp.stack(
        [
            block_maxima(ordered[local_index], first, share, block_rows)
            for local_index in range(CL_OWN)
        ]
    )
    whole = lax.all_gather(halves[:, :, None, :], "tile", axis=2, tiled=True)
    maxima = whole.reshape(CL_OWN, longest)
    answers = lookup_maxima(maxima, arrived_ranks, longest)
    returned = lax.all_to_all(answers, "owner", split_axis=0, concat_axis=0, tiled=True)
    return returned.reshape(cluster_count * capacity)[slot_index]


def local(embeddings, cluster_of, rank_of):
    count = lax.axis_size("owner") * lax.axis_size("tile")
    if (2 * embeddings.shape[0] // count) % 16 == 0:
        return fused(embeddings, cluster_of, rank_of, count)
    return exchanged(embeddings, cluster_of, rank_of)


def solution(mesh):
    in_specs = (
        P(("groups", "owner", "tile"), None),
        P(("groups", "owner", "tile")),
        P(("groups", "owner", "tile")),
    )
    out_specs = P(("groups", "owner", "tile"))
    return jax.shard_map(local, mesh=mesh, in_specs=in_specs, out_specs=out_specs, check_vma=False)
```

```python
import functools

import jax
import jax.numpy as jnp
from jax import lax
from jax.experimental import pallas as pl
from jax.experimental.pallas import tpu as pltpu
from jax.sharding import PartitionSpec as P

MESH = pl.DeviceIdType.MESH
EPSILON = 1e-06
LANES = 128


def flip(value, mask):
    bit = 1
    while bit <= mask:
        if mask & bit:
            value = value + bit * (1 - 2 * ((value // bit) % 2))
        bit *= 2
    return value


def cluster_kernel(
    count,
    capacity,
    emb_hbm,
    cluster_hbm,
    rank_hbm,
    out_ref,
    emb_ref,
    cluster_ref,
    rank_ref,
    send_rows,
    rows,
    normed,
    send_ranks,
    ranks,
    send_best,
    best,
    load_sem,
    row_send_sem,
    row_recv_sem,
    rank_send_sem,
    rank_recv_sem,
    best_send_sem,
    best_recv_sem,
):
    row_count, width = emb_ref.shape
    slots = count * capacity
    per = LANES // capacity
    blocks = slots // LANES
    owner = lax.axis_index("owner")
    core = lax.axis_index("tile")
    me = owner * 2 + core

    def peer(k):
        return {"owner": flip(owner, k // 2), "tile": flip(core, k % 2)}

    loads = [
        pltpu.make_async_copy(source, target, load_sem.at[i])
        for i, (source, target) in enumerate(
            [(cluster_hbm, cluster_ref), (rank_hbm, rank_ref), (emb_hbm, emb_ref)]
        )
    ]
    barrier = pltpu.get_barrier_semaphore()
    for k in range(count - 1, 0, -1):
        pl.semaphore_signal(barrier, inc=1, device_id=peer(k), device_id_type=MESH)
    for load in loads:
        load.start()

    loads[0].wait()
    cluster = cluster_ref[...].reshape(1, row_count)
    distance = cluster ^ me
    member = distance == lax.broadcasted_iota(jnp.int32, (count, row_count), 0)
    member_f = member.astype(jnp.float32)
    member_b = member_f.astype(jnp.bfloat16)
    before = (
        (
            lax.broadcasted_iota(jnp.int32, (row_count, row_count), 0)
            < lax.broadcasted_iota(jnp.int32, (row_count, row_count), 1)
        )
        .astype(jnp.float32)
        .astype(jnp.bfloat16)
    )
    seen = jnp.dot(member_b, before, preferred_element_type=jnp.float32)
    occurrence = jnp.sum(seen * member_f, axis=0, keepdims=True).astype(jnp.int32)
    slot = distance * capacity + occurrence
    nt = (((1,), (1,)), ((), ()))

    def block_rows(b, n=1):
        return pl.ds(b * LANES, n * LANES)

    def place(b, n=1):
        size = n * LANES
        chosen = slot == b * LANES + lax.broadcasted_iota(jnp.int32, (size, row_count), 0)
        chosen = chosen.astype(jnp.float32).astype(jnp.bfloat16)
        placed = jnp.dot(chosen, normed[...], preferred_element_type=jnp.float32)
        send_rows[block_rows(b, n)] = placed.astype(jnp.bfloat16)

    def row_copy(k):
        here = pl.ds(k * capacity, capacity)
        return pltpu.make_async_remote_copy(
            src_ref=send_rows.at[here],
            dst_ref=rows.at[here],
            send_sem=row_send_sem.at[k],
            recv_sem=row_recv_sem.at[k],
            device_id=peer(k),
            device_id_type=MESH,
        )

    def rank_copy(k):
        return pltpu.make_async_remote_copy(
            src_ref=send_ranks.at[k],
            dst_ref=ranks.at[k],
            send_sem=rank_send_sem.at[k],
            recv_sem=rank_recv_sem.at[k],
            device_id=peer(k),
            device_id_type=MESH,
        )

    def best_copy(k):
        return pltpu.make_async_remote_copy(
            src_ref=send_best.at[k // per],
            dst_ref=best.at[k],
            send_sem=best_send_sem.at[k],
            recv_sem=best_recv_sem.at[k],
            device_id=peer(k),
            device_id_type=MESH,
        )

    def start_rows(b):
        for k in range((b + 1) * per - 1, b * per - 1, -1):
            if k:
                row_copy(k).start()

    loads[1].wait()
    rank = rank_ref[...].reshape(1, row_count)
    lane_of = (slot % LANES) == lax.broadcasted_iota(jnp.int32, (LANES, row_count), 0)
    lane_b = lane_of.astype(jnp.float32).astype(jnp.bfloat16)
    high = (rank // 16 - slots // 16).astype(jnp.float32)
    low = (rank % 16).astype(jnp.float32)
    rank_high = lax.dot_general(
        (member_f * high).astype(jnp.bfloat16), lane_b, nt, preferred_element_type=jnp.float32
    )
    rank_low = lax.dot_general(
        (member_f * low).astype(jnp.bfloat16), lane_b, nt, preferred_element_type=jnp.float32
    )
    rank_rows = 16.0 * rank_high + rank_low
    for k in range(count):
        send_ranks[k] = rank_rows[k : k + 1, :]
    ranks[0] = rank_rows[0:1, :]

    loads[2].wait()
    values = emb_ref[...].astype(jnp.float32)
    total = jnp.sum(values * values, axis=1, keepdims=True)
    normed[...] = (values * lax.rsqrt(total + EPSILON)).astype(jnp.bfloat16)
    place(blocks - 1)
    pl.semaphore_wait(barrier, count - 1)
    for k in range(count - 1, 0, -1):
        rank_copy(k).start()
    place(blocks - 2)
    for j in range(per - 1, -1, -1):
        row_copy((blocks - 1) * per + j).start()
        row_copy((blocks - 2) * per + j).start()

    place(0, blocks - 2)
    for b in range(blocks - 3, -1, -1):
        start_rows(b)
    rows[:capacity] = send_rows[:capacity]

    def arrive(b, n=1):
        for k in range((b + n) * per - 1, b * per - 1, -1):
            if k:
                row_copy(k).wait_recv()

    for k in range(1, count):
        rank_copy(k).wait_recv()
    rank_lanes = [
        sum(ranks[b * per + j] for j in range(per)) + float(slots) for b in range(blocks)
    ]
    turned = jnp.transpose(
        jnp.concatenate(rank_lanes + [jnp.zeros((LANES - blocks, LANES), jnp.float32)], axis=0)
    )
    tops = [jnp.full((1, LANES), -1.0, jnp.float32) for _ in range(blocks)]

    def score(first_key, keys, first_query, queries):
        scores = lax.dot_general(
            rows[block_rows(first_key, keys)],
            rows[block_rows(first_query, queries)],
            nt,
            preferred_element_type=jnp.float32,
        )
        for q in range(queries):
            for b in range(keys):
                part = scores[b * LANES : (b + 1) * LANES, q * LANES : (q + 1) * LANES]
                key = first_key + b
                query = first_query + q
                earlier = turned[:, key : key + 1] < rank_lanes[query]
                found = jnp.max(jnp.where(earlier, part, -1.0), axis=0, keepdims=True)
                tops[query] = jnp.maximum(tops[query], found)

    def answer(b):
        send_best[b] = tops[b]
        for k in range((b + 1) * per - 1, b * per - 1, -1):
            if k:
                best_copy(k).start()
            else:
                best[0] = tops[b]

    near = blocks - 2
    arrive(0, near)
    score(0, near, 0, near)
    arrive(near + 1)
    score(0, near, near + 1, 1)
    score(near + 1, 1, near + 1, 1)
    score(near + 1, 1, 0, near)
    arrive(near)
    score(near, 1, near + 1, 1)
    answer(near + 1)
    score(0, blocks, near, 1)
    answer(near)
    score(near, 1, 0, near)
    for b in range(near - 1, -1, -1):
        answer(b)

    for k in range(1, count):
        row_copy(k).wait_send()
        rank_copy(k).wait_send()
    for k in range(1, count):
        best_copy(k).wait_send()
    for k in range(1, count):
        best_copy(k).wait_recv()
    answers = jnp.concatenate([best[k] for k in range(count)], axis=0)
    turned_answers = jnp.transpose(answers)
    parts = []
    for _ in range(3):
        part = turned_answers.astype(jnp.bfloat16)
        turned_answers = turned_answers - part.astype(jnp.float32)
        parts.append(jnp.dot(part, member_b, preferred_element_type=jnp.float32))
    spread = (parts[2] + parts[1]) + parts[0]
    picked = jnp.sum(jnp.where(lane_of, spread, 0.0), axis=0, keepdims=True)
    out_ref[...] = picked.reshape(row_count)


def fused(embeddings, cluster_of, rank_of, count):
    row_count, width = embeddings.shape
    capacity = 2 * row_count // count
    slots = count * capacity
    return pl.pallas_call(
        functools.partial(cluster_kernel, count, capacity),
        out_shape=jax.ShapeDtypeStruct((row_count,), jnp.float32),
        in_specs=[pl.BlockSpec(memory_space=pl.ANY)] * 3,
        out_specs=pl.BlockSpec(memory_space=pltpu.VMEM),
        scratch_shapes=[
            pltpu.VMEM((row_count, width), jnp.bfloat16),
            pltpu.VMEM((row_count,), jnp.int32),
            pltpu.VMEM((row_count,), jnp.int32),
            pltpu.VMEM((slots, width), jnp.bfloat16),
            pltpu.VMEM((slots, width), jnp.bfloat16),
            pltpu.VMEM((row_count, width), jnp.bfloat16),
            pltpu.VMEM((count, 1, LANES), jnp.float32),
            pltpu.VMEM((count, 1, LANES), jnp.float32),
            pltpu.VMEM((slots // LANES, 1, LANES), jnp.float32),
            pltpu.VMEM((count, 1, LANES), jnp.float32),
            pltpu.SemaphoreType.DMA((3,)),
        ]
        + [pltpu.SemaphoreType.DMA((count,))] * 6,
        compiler_params=pltpu.CompilerParams(collective_id=0, has_side_effects=True),
    )(embeddings, cluster_of, rank_of)


CL_OWN = 2


def normalize_rows(embeddings):
    as_float = embeddings.astype(jnp.float32)
    total = jnp.sum(as_float * as_float, axis=1, keepdims=True)
    return (as_float * lax.rsqrt(total + EPSILON)).astype(jnp.bfloat16)


def place_rows(arrived_rows, arrived_ranks, longest):
    local_count = arrived_rows.shape[1]
    feature_width = arrived_rows.shape[3]
    cluster_index = jnp.broadcast_to(
        jnp.arange(local_count, dtype=jnp.int32)[None, :, None], arrived_ranks.shape
    )
    ordered = jnp.zeros((local_count, longest, feature_width), jnp.bfloat16)
    ordered = ordered.at[cluster_index, arrived_ranks].set(arrived_rows, mode="drop")
    live_rows = jnp.sum((arrived_ranks < longest).astype(jnp.int32), axis=(0, 2))
    return (ordered, live_rows)


def lookup_maxima(maxima, ranks, longest):
    cluster_index = jnp.broadcast_to(
        jnp.arange(maxima.shape[0], dtype=jnp.int32)[None, :, None], ranks.shape
    )
    return maxima[cluster_index, jnp.minimum(ranks, longest - 1)]


def block_maxima(ordered_rows, first, count, block_rows):
    query_rows = lax.dynamic_slice_in_dim(ordered_rows, 0 + first, count, 0)
    scores = jnp.einsum("qd,kd->qk", query_rows, ordered_rows, preferred_element_type=jnp.float32)
    query_pos = 0 + first + jnp.arange(count, dtype=jnp.int32)
    key_pos = jnp.arange(block_rows, dtype=jnp.int32)
    masked = jnp.where(key_pos[None, :] < query_pos[:, None], scores, -1.0)
    row_best = jnp.max(masked, axis=1)
    results = [row_best]
    return jnp.stack(results)


def exchanged(embeddings, cluster_of, rank_of):
    row_count, feature_width = embeddings.shape
    owner_count = lax.axis_size("owner")
    core_count = lax.axis_size("tile")
    cluster_count = CL_OWN * owner_count
    capacity = 2 * row_count // cluster_count
    longest = owner_count * core_count * capacity
    block_rows = 512
    normed = normalize_rows(embeddings)
    member = (cluster_of[:, None] == jnp.arange(cluster_count, dtype=jnp.int32)[None, :]).astype(
        jnp.bfloat16
    )
    row_ids = jnp.arange(row_count, dtype=jnp.int32)
    earlier = (row_ids[:, None] > row_ids[None, :]).astype(jnp.bfloat16)
    seen = jnp.dot(earlier, member, preferred_element_type=jnp.float32)
    occurrence = jnp.sum(seen * member.astype(jnp.float32), axis=1).astype(jnp.int32)
    slot_index = cluster_of * capacity + occurrence
    outgoing = (
        jnp.zeros((cluster_count * capacity, feature_width), jnp.bfloat16)
        .at[slot_index]
        .set(normed)
    )
    outgoing_ranks = (
        jnp.full((cluster_count * capacity,), longest, jnp.int32).at[slot_index].set(rank_of)
    )
    outgoing = outgoing.reshape(owner_count, CL_OWN, capacity, feature_width)
    outgoing_ranks = outgoing_ranks.reshape(owner_count, CL_OWN, capacity)
    arrived, arrived_ranks = (
        lax.all_to_all(outgoing, "owner", split_axis=0, concat_axis=0, tiled=True),
        lax.all_to_all(outgoing_ranks, "owner", split_axis=0, concat_axis=0, tiled=True),
    )
    everything, every_rank = (
        lax.all_gather(arrived, "tile", axis=0, tiled=True),
        lax.all_gather(arrived_ranks, "tile", axis=0, tiled=True),
    )
    ordered, live_rows = place_rows(everything, every_rank, longest)
    share = block_rows // core_count
    first = lax.axis_index("tile") * share
    halves = jnp.stack(
        [
            block_maxima(ordered[local_index], first, share, block_rows)
            for local_index in range(CL_OWN)
        ]
    )
    whole = lax.all_gather(halves[:, :, None, :], "tile", axis=2, tiled=True)
    maxima = whole.reshape(CL_OWN, longest)
    answers = lookup_maxima(maxima, arrived_ranks, longest)
    returned = lax.all_to_all(answers, "owner", split_axis=0, concat_axis=0, tiled=True)
    return returned.reshape(cluster_count * capacity)[slot_index]


def local(embeddings, cluster_of, rank_of):
    count = lax.axis_size("owner") * lax.axis_size("tile")
    if (2 * embeddings.shape[0] // count) % 16 == 0:
        return fused(embeddings, cluster_of, rank_of, count)
    return exchanged(embeddings, cluster_of, rank_of)


def solution(mesh):
    in_specs = (
        P(("groups", "owner", "tile"), None),
        P(("groups", "owner", "tile")),
        P(("groups", "owner", "tile")),
    )
    out_specs = P(("groups", "owner", "tile"))
    return jax.shard_map(local, mesh=mesh, in_specs=in_specs, out_specs=out_specs, check_vma=False)
```

```python
import functools

import jax
import jax.numpy as jnp
from jax import lax
from jax.experimental import pallas as pl
from jax.experimental.pallas import tpu as pltpu
from jax.sharding import PartitionSpec as P

MESH = pl.DeviceIdType.MESH
EPSILON = 1e-06
LANES = 128


def flip(value, mask):
    bit = 1
    while bit <= mask:
        if mask & bit:
            value = value + bit * (1 - 2 * ((value // bit) % 2))
        bit *= 2
    return value


def cluster_kernel(
    count,
    capacity,
    emb_hbm,
    cluster_hbm,
    rank_hbm,
    out_ref,
    emb_ref,
    cluster_ref,
    rank_ref,
    send_rows,
    rows,
    normed,
    send_ranks,
    ranks,
    send_best,
    best,
    load_sem,
    row_send_sem,
    row_recv_sem,
    rank_send_sem,
    rank_recv_sem,
    best_send_sem,
    best_recv_sem,
):
    row_count, width = emb_ref.shape
    slots = count * capacity
    per = LANES // capacity
    blocks = slots // LANES
    owner = lax.axis_index("owner")
    core = lax.axis_index("tile")
    me = owner * 2 + core

    def peer(k):
        return {"owner": flip(owner, k // 2), "tile": flip(core, k % 2)}

    loads = [
        pltpu.make_async_copy(source, target, load_sem.at[i])
        for i, (source, target) in enumerate(
            [(cluster_hbm, cluster_ref), (rank_hbm, rank_ref), (emb_hbm, emb_ref)]
        )
    ]
    barrier = pltpu.get_barrier_semaphore()
    for k in range(count - 1, 0, -1):
        pl.semaphore_signal(barrier, inc=1, device_id=peer(k), device_id_type=MESH)
    for load in loads:
        load.start()

    loads[0].wait()
    cluster = cluster_ref[...].reshape(1, row_count)
    distance = cluster ^ me
    member = distance == lax.broadcasted_iota(jnp.int32, (count, row_count), 0)
    member_f = member.astype(jnp.float32)
    member_b = member_f.astype(jnp.bfloat16)
    before = (
        (
            lax.broadcasted_iota(jnp.int32, (row_count, row_count), 0)
            < lax.broadcasted_iota(jnp.int32, (row_count, row_count), 1)
        )
        .astype(jnp.float32)
        .astype(jnp.bfloat16)
    )
    seen = jnp.dot(member_b, before, preferred_element_type=jnp.float32)
    occurrence = jnp.sum(seen * member_f, axis=0, keepdims=True).astype(jnp.int32)
    slot = distance * capacity + occurrence
    nt = (((1,), (1,)), ((), ()))

    def block_rows(b, n=1):
        return pl.ds(b * LANES, n * LANES)

    def place(b, n=1):
        size = n * LANES
        chosen = slot == b * LANES + lax.broadcasted_iota(jnp.int32, (size, row_count), 0)
        chosen = chosen.astype(jnp.float32).astype(jnp.bfloat16)
        placed = jnp.dot(chosen, normed[...], preferred_element_type=jnp.float32)
        send_rows[block_rows(b, n)] = placed.astype(jnp.bfloat16)

    def row_copy(k):
        here = pl.ds(k * capacity, capacity)
        return pltpu.make_async_remote_copy(
            src_ref=send_rows.at[here],
            dst_ref=rows.at[here],
            send_sem=row_send_sem.at[k],
            recv_sem=row_recv_sem.at[k],
            device_id=peer(k),
            device_id_type=MESH,
        )

    def rank_copy(k):
        return pltpu.make_async_remote_copy(
            src_ref=send_ranks.at[k],
            dst_ref=ranks.at[k],
            send_sem=rank_send_sem.at[k],
            recv_sem=rank_recv_sem.at[k],
            device_id=peer(k),
            device_id_type=MESH,
        )

    def best_copy(k):
        return pltpu.make_async_remote_copy(
            src_ref=send_best.at[k // per],
            dst_ref=best.at[k],
            send_sem=best_send_sem.at[k],
            recv_sem=best_recv_sem.at[k],
            device_id=peer(k),
            device_id_type=MESH,
        )

    def start_rows(b):
        for k in range((b + 1) * per - 1, b * per - 1, -1):
            if k:
                row_copy(k).start()

    loads[1].wait()
    rank = rank_ref[...].reshape(1, row_count)
    lane_of = (slot % LANES) == lax.broadcasted_iota(jnp.int32, (LANES, row_count), 0)
    lane_b = lane_of.astype(jnp.float32).astype(jnp.bfloat16)
    high = (rank // 16 - slots // 16).astype(jnp.float32)
    low = (rank % 16).astype(jnp.float32)
    rank_high = lax.dot_general(
        (member_f * high).astype(jnp.bfloat16), lane_b, nt, preferred_element_type=jnp.float32
    )
    rank_low = lax.dot_general(
        (member_f * low).astype(jnp.bfloat16), lane_b, nt, preferred_element_type=jnp.float32
    )
    rank_rows = 16.0 * rank_high + rank_low
    for k in range(count):
        send_ranks[k] = rank_rows[k : k + 1, :]
    ranks[0] = rank_rows[0:1, :]

    loads[2].wait()
    values = emb_ref[...].astype(jnp.float32)
    total = jnp.sum(values * values, axis=1, keepdims=True)
    normed[...] = (values * lax.rsqrt(total + EPSILON)).astype(jnp.bfloat16)
    place(blocks - 2, 2)
    pl.semaphore_wait(barrier, count - 1)
    for k in range(count - 1, 0, -1):
        rank_copy(k).start()
    for j in range(per - 1, -1, -1):
        row_copy((blocks - 1) * per + j).start()
        row_copy((blocks - 2) * per + j).start()

    place(0, blocks - 2)
    for b in range(blocks - 3, -1, -1):
        start_rows(b)
    rows[:capacity] = send_rows[:capacity]

    def arrive(b, n=1):
        for k in range((b + n) * per - 1, b * per - 1, -1):
            if k:
                row_copy(k).wait_recv()

    for k in range(1, count):
        rank_copy(k).wait_recv()
    rank_lanes = [
        sum(ranks[b * per + j] for j in range(per)) + float(slots) for b in range(blocks)
    ]
    turned = jnp.transpose(
        jnp.concatenate(rank_lanes + [jnp.zeros((LANES - blocks, LANES), jnp.float32)], axis=0)
    )
    tops = [jnp.full((1, LANES), -1.0, jnp.float32) for _ in range(blocks)]

    def score(first_key, keys, first_query, queries):
        scores = lax.dot_general(
            rows[block_rows(first_key, keys)],
            rows[block_rows(first_query, queries)],
            nt,
            preferred_element_type=jnp.float32,
        )
        for q in range(queries):
            for b in range(keys):
                part = scores[b * LANES : (b + 1) * LANES, q * LANES : (q + 1) * LANES]
                key = first_key + b
                query = first_query + q
                earlier = turned[:, key : key + 1] < rank_lanes[query]
                found = jnp.max(jnp.where(earlier, part, -1.0), axis=0, keepdims=True)
                tops[query] = jnp.maximum(tops[query], found)

    def answer(b):
        send_best[b] = tops[b]
        for k in range((b + 1) * per - 1, b * per - 1, -1):
            if k:
                best_copy(k).start()
            else:
                best[0] = tops[b]

    near = blocks - 2
    arrive(0, near)
    score(0, near, 0, near)
    arrive(near + 1)
    score(0, near, near + 1, 1)
    score(near + 1, 1, near + 1, 1)
    score(near + 1, 1, 0, near)
    arrive(near)
    score(near, 1, near + 1, 1)
    answer(near + 1)
    score(0, blocks, near, 1)
    answer(near)
    score(near, 1, 0, near)
    for b in range(near - 1, -1, -1):
        answer(b)

    for k in range(1, count):
        row_copy(k).wait_send()
        rank_copy(k).wait_send()
    for k in range(1, count):
        best_copy(k).wait_send()
    for k in range(1, count):
        best_copy(k).wait_recv()
    answers = jnp.concatenate([best[k] for k in range(count)], axis=0)
    turned_answers = jnp.transpose(answers)
    parts = []
    for _ in range(3):
        part = turned_answers.astype(jnp.bfloat16)
        turned_answers = turned_answers - part.astype(jnp.float32)
        parts.append(jnp.dot(part, member_b, preferred_element_type=jnp.float32))
    spread = (parts[2] + parts[1]) + parts[0]
    picked = jnp.sum(jnp.where(lane_of, spread, 0.0), axis=0, keepdims=True)
    out_ref[...] = picked.reshape(row_count)


def fused(embeddings, cluster_of, rank_of, count):
    row_count, width = embeddings.shape
    capacity = 2 * row_count // count
    slots = count * capacity
    return pl.pallas_call(
        functools.partial(cluster_kernel, count, capacity),
        out_shape=jax.ShapeDtypeStruct((row_count,), jnp.float32),
        in_specs=[pl.BlockSpec(memory_space=pl.ANY)] * 3,
        out_specs=pl.BlockSpec(memory_space=pltpu.VMEM),
        scratch_shapes=[
            pltpu.VMEM((row_count, width), jnp.bfloat16),
            pltpu.VMEM((row_count,), jnp.int32),
            pltpu.VMEM((row_count,), jnp.int32),
            pltpu.VMEM((slots, width), jnp.bfloat16),
            pltpu.VMEM((slots, width), jnp.bfloat16),
            pltpu.VMEM((row_count, width), jnp.bfloat16),
            pltpu.VMEM((count, 1, LANES), jnp.float32),
            pltpu.VMEM((count, 1, LANES), jnp.float32),
            pltpu.VMEM((slots // LANES, 1, LANES), jnp.float32),
            pltpu.VMEM((count, 1, LANES), jnp.float32),
            pltpu.SemaphoreType.DMA((3,)),
        ]
        + [pltpu.SemaphoreType.DMA((count,))] * 6,
        compiler_params=pltpu.CompilerParams(collective_id=0, has_side_effects=True),
    )(embeddings, cluster_of, rank_of)


CL_OWN = 2


def normalize_rows(embeddings):
    as_float = embeddings.astype(jnp.float32)
    total = jnp.sum(as_float * as_float, axis=1, keepdims=True)
    return (as_float * lax.rsqrt(total + EPSILON)).astype(jnp.bfloat16)


def place_rows(arrived_rows, arrived_ranks, longest):
    local_count = arrived_rows.shape[1]
    feature_width = arrived_rows.shape[3]
    cluster_index = jnp.broadcast_to(
        jnp.arange(local_count, dtype=jnp.int32)[None, :, None], arrived_ranks.shape
    )
    ordered = jnp.zeros((local_count, longest, feature_width), jnp.bfloat16)
    ordered = ordered.at[cluster_index, arrived_ranks].set(arrived_rows, mode="drop")
    live_rows = jnp.sum((arrived_ranks < longest).astype(jnp.int32), axis=(0, 2))
    return (ordered, live_rows)


def lookup_maxima(maxima, ranks, longest):
    cluster_index = jnp.broadcast_to(
        jnp.arange(maxima.shape[0], dtype=jnp.int32)[None, :, None], ranks.shape
    )
    return maxima[cluster_index, jnp.minimum(ranks, longest - 1)]


def block_maxima(ordered_rows, first, count, block_rows):
    query_rows = lax.dynamic_slice_in_dim(ordered_rows, 0 + first, count, 0)
    scores = jnp.einsum("qd,kd->qk", query_rows, ordered_rows, preferred_element_type=jnp.float32)
    query_pos = 0 + first + jnp.arange(count, dtype=jnp.int32)
    key_pos = jnp.arange(block_rows, dtype=jnp.int32)
    masked = jnp.where(key_pos[None, :] < query_pos[:, None], scores, -1.0)
    row_best = jnp.max(masked, axis=1)
    results = [row_best]
    return jnp.stack(results)


def exchanged(embeddings, cluster_of, rank_of):
    row_count, feature_width = embeddings.shape
    owner_count = lax.axis_size("owner")
    core_count = lax.axis_size("tile")
    cluster_count = CL_OWN * owner_count
    capacity = 2 * row_count // cluster_count
    longest = owner_count * core_count * capacity
    block_rows = 512
    normed = normalize_rows(embeddings)
    member = (cluster_of[:, None] == jnp.arange(cluster_count, dtype=jnp.int32)[None, :]).astype(
        jnp.bfloat16
    )
    row_ids = jnp.arange(row_count, dtype=jnp.int32)
    earlier = (row_ids[:, None] > row_ids[None, :]).astype(jnp.bfloat16)
    seen = jnp.dot(earlier, member, preferred_element_type=jnp.float32)
    occurrence = jnp.sum(seen * member.astype(jnp.float32), axis=1).astype(jnp.int32)
    slot_index = cluster_of * capacity + occurrence
    outgoing = (
        jnp.zeros((cluster_count * capacity, feature_width), jnp.bfloat16)
        .at[slot_index]
        .set(normed)
    )
    outgoing_ranks = (
        jnp.full((cluster_count * capacity,), longest, jnp.int32).at[slot_index].set(rank_of)
    )
    outgoing = outgoing.reshape(owner_count, CL_OWN, capacity, feature_width)
    outgoing_ranks = outgoing_ranks.reshape(owner_count, CL_OWN, capacity)
    arrived, arrived_ranks = (
        lax.all_to_all(outgoing, "owner", split_axis=0, concat_axis=0, tiled=True),
        lax.all_to_all(outgoing_ranks, "owner", split_axis=0, concat_axis=0, tiled=True),
    )
    everything, every_rank = (
        lax.all_gather(arrived, "tile", axis=0, tiled=True),
        lax.all_gather(arrived_ranks, "tile", axis=0, tiled=True),
    )
    ordered, live_rows = place_rows(everything, every_rank, longest)
    share = block_rows // core_count
    first = lax.axis_index("tile") * share
    halves = jnp.stack(
        [
            block_maxima(ordered[local_index], first, share, block_rows)
            for local_index in range(CL_OWN)
        ]
    )
    whole = lax.all_gather(halves[:, :, None, :], "tile", axis=2, tiled=True)
    maxima = whole.reshape(CL_OWN, longest)
    answers = lookup_maxima(maxima, arrived_ranks, longest)
    returned = lax.all_to_all(answers, "owner", split_axis=0, concat_axis=0, tiled=True)
    return returned.reshape(cluster_count * capacity)[slot_index]


def local(embeddings, cluster_of, rank_of):
    count = lax.axis_size("owner") * lax.axis_size("tile")
    if (2 * embeddings.shape[0] // count) % 16 == 0:
        return fused(embeddings, cluster_of, rank_of, count)
    return exchanged(embeddings, cluster_of, rank_of)


def solution(mesh):
    in_specs = (
        P(("groups", "owner", "tile"), None),
        P(("groups", "owner", "tile")),
        P(("groups", "owner", "tile")),
    )
    out_specs = P(("groups", "owner", "tile"))
    return jax.shard_map(local, mesh=mesh, in_specs=in_specs, out_specs=out_specs, check_vma=False)
```
